32 devices in a mesh: groups: 2 (over x), ctx: 16 (over z, y, core).
Axes of the slice: x: 2, y: 2, z: 4, core: 2. Of those that a mesh axis runs over, the one named last changes fastest.
Arguments:
- residual: bfloat16 [2048, 3072], P(('groups', 'ctx')), parts along dimension 0, may hold values from -36 to 36
- queries: bfloat16 [2048, 3072], P(('groups', 'ctx')), parts along dimension 0, may hold values from -112 to 112
- keys: bfloat16 [2048, 512], P(('groups', 'ctx')), parts along dimension 0, may hold values from -4 to 4
- values: bfloat16 [2048, 512], P(('groups', 'ctx')), parts along dimension 0, may hold values from -6 to 6
- block_order: int32 [64], P('groups'), parts along dimension 0, may hold values from 0 to 31, each once
- expert_ids: int32 [2048, 1], P(('groups', 'ctx')), parts along dimension 0, may hold values from 0 to 3; in each aligned block of 64 rows (0 to 63, 64 to 127, ...) at most 18 rows name the same one
- router: bfloat16 [3072, 4], replicated, may hold values from -0.109375 to 0.109375
- w_gate: bfloat16 [16, 3072, 2048], P('ctx'), may hold values from -0.109375 to 0.109375
- w_up: bfloat16 [16, 3072, 2048], P('ctx'), may hold values from -0.109375 to 0.109375
- w_down: bfloat16 [16, 2048, 3072], P('ctx'), may hold values from -0.0625 to 0.0625
Outputs:
- attended: bfloat16 [2048, 3072], P(('groups', 'ctx')), parts along dimension 0
- mixed: bfloat16 [2048, 3072], P(('groups', 'ctx')), parts along dimension 0
The draws below stay inside these ranges and needn't reach their ends.
There are 2 independent parts, one for each index of `groups`. The reference program is written for one: setup_inputs(seed, part) draws one part's arguments, and reference() takes and returns one part's arrays. A program takes and returns all parts, laid end to end along the dimension named above; an argument that names none is the same for every part. Nothing has to cross between parts.
Inputs may be any that keep to these rules, and one draw needn't show every extreme that they name: `expert_ids`: within the 64 rows of one device no expert is named by more than 18 rows, a bound that some block reaches. `block_order`: every half-block of the sequence stands once.
All inputs are finite; a program needn't handle non-finite values.
Results may differ from the reference program's by a relative error of at most 0.0095.
Values may be sent and summed in bfloat16 or wider, within the bound.
A program may use at most 128 MiB of HBM per device.

```python
import math
import jax
import jax.numpy as jnp
import numpy as np
from jax import lax

HEADS = 24
KV_HEADS = 4
HEAD_DIM = 128
D = 3072
EXPERTS = 4
TOPK = 1
HID = 8192
TOK_DEV = 64
TOKENS = 1024
HALF = 32
REP = 4
MOST = 18
N_CTX = 16


def key_base(key):
    return jnp.clip(jax.random.normal(jax.random.fold_in(key, 7), (TOKENS, KV_HEADS * HEAD_DIM), jnp.float32), -4.0, 4.0)


def draw_residual(key, part):
    key = jax.random.fold_in(key, 1)
    first, second, third = jax.random.split(key, 3)
    base = jnp.clip(jax.random.normal(first, (TOKENS, D), jnp.float32), -4.0, 4.0)
    row_scale = jnp.exp(jax.random.uniform(second, (TOKENS, 1), jnp.float32, math.log(0.3), math.log(3.0)))
    col_scale = jnp.exp(jax.random.uniform(third, (1, D), jnp.float32, math.log(0.3), math.log(3.0)))
    return (base * row_scale * col_scale).astype(jnp.bfloat16)


def draw_keys(key, part):
    base = key_base(key)
    return base.astype(jnp.bfloat16)


def draw_queries(key, part):
    key = jax.random.fold_in(key, 3)
    fresh = jnp.clip(2.5 * jax.random.normal(key, (TOKENS, D), jnp.float32), -10.0, 10.0)
    return fresh.astype(jnp.bfloat16)


def levels(own_key, dims, cuts, smallest, high):
    factor_of, own = 1.0, jax.random.fold_in(own_key, 6)
    for axis_at, shards_of in cuts:
        draws = jnp.exp(jax.random.uniform(jax.random.fold_in(own, axis_at), (shards_of,), jnp.float32, smallest / len(cuts), high / len(cuts)))
        factor_of = factor_of * jnp.repeat(draws, dims[axis_at] // shards_of).reshape([-1 if axis == axis_at else 1 for axis in range(len(dims))])
    return factor_of


def routed_block(rng, own, number, rows, number_of, top, most, skew):
    sequence = jax.random.permutation(rng, number_of)
    packed, usual = shares(number_of, rows * top, most, skew, True), shares(number_of, rows * top, most, skew, False)
    places = jnp.arange(number_of)

    def named(lengths, turn):
        used = int((lengths > 0).sum())
        fixed = max(1, used // 4)
        passed = fixed + (places - fixed + turn * (used - fixed)) % max(1, number_of - fixed)
        return jnp.zeros((number_of,), jnp.int32).at[sequence[jnp.where(places < fixed, places, passed)]].set(jnp.asarray(lengths, jnp.int32))

    lengths = jnp.where(number % 4 == 0, named(packed, number // 4), named(usual, number - number // 4 - 1))
    mixed = jax.random.permutation(jax.random.fold_in(own, 3), number_of)
    source_of, receiver = mixed[0:number_of // 2 * 2:2], mixed[1:number_of // 2 * 2:2]
    room = jnp.minimum(lengths[source_of] - 1, most - lengths[receiver]) // 2
    room = jnp.where((source_of == sequence[0]) | (receiver == sequence[0]) | (lengths[receiver] == 0), 0, jnp.maximum(room, 0))
    passed = jax.random.randint(jax.random.fold_in(own, 4), (number_of // 2,), 0, 1 << 20) % (room + 1)
    lengths = lengths.at[source_of].add(-passed).at[receiver].add(passed)
    labels = jnp.searchsorted(jnp.cumsum(lengths), jnp.arange(rows * top), side="right").astype(jnp.int32)
    listing = labels.reshape(top, rows).T
    listing = listing[jax.random.permutation(jax.random.fold_in(own, 1), rows)]
    turn = jax.random.randint(jax.random.fold_in(own, 2), (rows, 1), 0, top)
    return jnp.take_along_axis(listing, (jnp.arange(top)[None, :] + turn) % top, axis=1)


def shares(count, total, limit, slope, full):
    loads = [(1 << 20) // math.isqrt(standing ** slope) + 1 for standing in range(1, count + 1)]
    largest = limit if full else min(limit, max(-(-total // count), total * loads[0] // sum(loads)))
    least = 1 if total - largest >= count - 1 else 0
    counts, rest = [largest] + [least] * (count - 1), total - largest - least * (count - 1)
    while rest > 0:
        movable = [i for i in range(1, count) if counts[i] < largest] or [i for i in range(1, count) if counts[i] < limit]
        pool, remaining = sum([loads[i] for i in movable]), rest
        for i in movable:
            extra = min(limit - counts[i], max(1, remaining * loads[i] // pool), rest)
            counts[i] = counts[i] + extra
            rest = rest - extra
    return np.array(counts)


def gaussian(own_key, shape, width, most, pieces=(), held_as=jnp.bfloat16):
    drawn = jax.random.normal(own_key, shape, jnp.float32) * width
    if len(pieces) > 0:
        drawn = levels(own_key, shape, pieces, -0.22, 0.18) * drawn
    return jnp.clip(drawn, min=-most, max=most).astype(held_as)


def setup_inputs(seed: int = 0, part: int = 0) -> dict:
    arg_keys = jax.random.split(jax.random.key(seed), 11)
    part_splits = jax.random.split(jax.random.fold_in(arg_keys[10], part), 11)
    residual = draw_residual(jax.random.fold_in(jax.random.fold_in(arg_keys[10], part), 71), part)
    queries = draw_queries(jax.random.fold_in(jax.random.fold_in(arg_keys[10], part), 71), part)
    keys = draw_keys(jax.random.fold_in(jax.random.fold_in(arg_keys[10], part), 71), part)
    values = gaussian(part_splits[3], (TOKENS, KV_HEADS * HEAD_DIM), 1.0, 6.0, ((0, 16),))
    block_order = jax.random.permutation(part_splits[4], 2 * N_CTX).astype(jnp.int32)
    expert_ids_keys = jax.random.split(jax.random.fold_in(part_splits[5], 1), TOKENS // TOK_DEV)
    expert_ids_turns = jax.random.permutation(jax.random.fold_in(part_splits[5], 3), TOKENS // TOK_DEV)
    expert_ids = jax.vmap(lambda own, number: routed_block(jax.random.fold_in(part_splits[5], 2), own, number, TOK_DEV, EXPERTS, TOPK, MOST, 2))(expert_ids_keys, expert_ids_turns).reshape((TOKENS, TOPK))
    router = gaussian(arg_keys[6], (D, EXPERTS), D ** -0.5, 0.109375)
    w_gate = gaussian(arg_keys[7], (N_CTX, D, HID // REP), D ** -0.5, 0.109375, ((0, 16),))
    w_up = gaussian(arg_keys[8], (N_CTX, D, HID // REP), D ** -0.5, 0.109375, ((0, 16),))
    w_down = gaussian(arg_keys[9], (N_CTX, HID // REP, D), HID ** -0.5, 0.0625, ((0, 16),))
    return dict(residual=residual, queries=queries, keys=keys, values=values, block_order=block_order, expert_ids=expert_ids, router=router, w_gate=w_gate, w_up=w_up, w_down=w_down)


def reference(residual, queries, keys, values, block_order, expert_ids, router, w_gate, w_up, w_down):
    rows = jnp.arange(TOKENS, dtype=jnp.int32)
    pos = (block_order[rows // HALF] * HALF + rows % HALF).astype(jnp.int32)
    group = HEADS // KV_HEADS
    scale = 1.0 / math.sqrt(HEAD_DIM)
    qall = queries.astype(jnp.float32).reshape(TOKENS, HEADS, HEAD_DIM)
    kall = keys.astype(jnp.float32).reshape(TOKENS, KV_HEADS, HEAD_DIM)
    vall = values.astype(jnp.float32).reshape(TOKENS, KV_HEADS, HEAD_DIM)
    qblock = math.gcd(TOKENS, 1024)
    nblocks = TOKENS // qblock

    def head_out(head):
        qhead = lax.dynamic_index_in_dim(qall, head, 1, keepdims=False)
        khead = lax.dynamic_index_in_dim(kall, head // group, 1, keepdims=False)
        vhead = lax.dynamic_index_in_dim(vall, head // group, 1, keepdims=False)

        def block(index):
            start = (index * qblock).astype(jnp.int32)
            qpart = lax.dynamic_slice_in_dim(qhead, start, qblock, 0)
            qpos = lax.dynamic_slice_in_dim(pos, start, qblock, 0)
            scores = jnp.dot(qpart, khead.T, precision=lax.Precision.HIGHEST) * scale
            keep = qpos[:, None] >= pos[None, :]
            masked = jnp.where(keep, scores, jnp.float32(-1e+30))
            top = lax.optimization_barrier(jnp.max(masked, axis=1, keepdims=True))
            weights = jnp.where(keep, jnp.exp(masked - top), jnp.float32(0.0))
            total = lax.optimization_barrier(jnp.sum(weights, axis=1, keepdims=True))
            probs = lax.optimization_barrier(weights.astype(jnp.bfloat16))
            summed = jnp.dot(probs.astype(jnp.float32), vhead, precision=lax.Precision.HIGHEST)
            return summed / total
        return lax.map(block, jnp.arange(nblocks, dtype=jnp.int32)).reshape(TOKENS, HEAD_DIM)
    heads_out = lax.map(head_out, jnp.arange(HEADS, dtype=jnp.int32))
    attended = jnp.transpose(heads_out, (1, 0, 2)).reshape(TOKENS, D).astype(jnp.bfloat16)
    stream = residual.astype(jnp.float32) + attended.astype(jnp.float32)
    normed = (stream * lax.rsqrt(lax.optimization_barrier(jnp.mean(stream * stream, axis=1, keepdims=True)) + 1e-05)).astype(jnp.bfloat16)
    logits = jnp.dot(normed, router, preferred_element_type=jnp.float32)
    chosen = jnp.take_along_axis(logits, expert_ids, axis=1)[:, 0]
    gate = 1.0 / lax.optimization_barrier(jnp.sum(jnp.exp(logits - chosen[:, None]), axis=1))
    bound = N_CTX * MOST

    def add_expert(expert, total):
        named = expert_ids[:, 0] == expert
        share = jnp.where(named, gate, jnp.float32(0.0))
        count = jnp.sum(named.astype(jnp.int32))
        where_rows = jnp.nonzero(named, size=bound, fill_value=0)[0].astype(jnp.int32)
        valid = jnp.arange(bound, dtype=jnp.int32) < count
        picked = jnp.take(normed, where_rows, axis=0)

        def add_slice(index, acc):
            owner = (expert * REP + index).astype(jnp.int32)
            gate_w = lax.dynamic_index_in_dim(w_gate, owner, 0, keepdims=False)
            up_w = lax.dynamic_index_in_dim(w_up, owner, 0, keepdims=False)
            down_w = lax.dynamic_index_in_dim(w_down, owner, 0, keepdims=False)
            gated = jnp.dot(picked, gate_w, preferred_element_type=jnp.float32)
            upper = jnp.dot(picked, up_w, preferred_element_type=jnp.float32)
            hidden = (jax.nn.silu(gated) * upper).astype(jnp.bfloat16)
            part = lax.optimization_barrier(jnp.dot(hidden, down_w, preferred_element_type=jnp.float32).astype(jnp.bfloat16))
            return acc + part.astype(jnp.float32)
        expert_out = lax.fori_loop(0, REP, add_slice, jnp.zeros((bound, D), jnp.float32))
        weight_rows = jnp.where(valid, jnp.take(share, where_rows, axis=0), jnp.float32(0.0))
        return total.at[where_rows].add(weight_rows[:, None] * expert_out)
    mixed = lax.fori_loop(0, EXPERTS, add_expert, jnp.zeros((TOKENS, D), jnp.float32))
    return (attended, mixed.astype(jnp.bfloat16))
```

```python
import functools
import math

import jax
import jax.numpy as jnp
from jax import lax
from jax.experimental import pallas as pl
from jax.experimental.pallas import tpu as pltpu
from jax.sharding import PartitionSpec as P

HEAD_DIM = 128
MOST = 18
MAIN = 16
EXT = MOST - MAIN
SEGS = MAIN // EXT
CHUNKS = 3
MESH = pl.DeviceIdType.MESH
BF = jnp.bfloat16
F32 = jnp.float32


def dot(a, b):
    return jnp.dot(a, b, preferred_element_type=F32)


def dot_rows(a, b):
    return lax.dot_general(a, b, (((0,), (0,)), ((), ())), preferred_element_type=F32)


def dot_lanes(a, b):
    return lax.dot_general(a, b, (((1,), (1,)), ((), ())), preferred_element_type=F32)


def iota(shape, axis):
    return lax.broadcasted_iota(jnp.int32, shape, axis)


def fold(wide, pieces):
    width = wide.shape[1] // pieces
    return jnp.concatenate([wide[:, j * width : (j + 1) * width] for j in range(pieces)], axis=0)


def unfold(tall, pieces):
    rows = tall.shape[0] // pieces
    return jnp.concatenate([tall[j * rows : (j + 1) * rows] for j in range(pieces)], axis=1)


def kernel(
    count,
    experts,
    residual,
    queries,
    keys,
    values,
    order,
    ids,
    router_t,
    w_gate,
    w_up,
    w_down,
    attended,
    mixed,
    gate_w,
    up_w,
    down_w,
    kv,
    outbox,
    lists,
    gated,
    upper,
    hidden,
    part,
    from_pair,
    to_group,
    from_group,
    total,
    final,
    weight_sem,
    group_sem,
    pair_sem,
    back_pair_sem,
    back_group_sem,
    back_sem,
):
    tokens, width = queries.shape
    kv_width = keys.shape[1]
    kv_heads = kv_width // HEAD_DIM
    group = width // kv_width
    half_rows = tokens // 2
    reps = count // experts
    halves = reps // 2
    chunk = width // CHUNKS
    seg = chunk // SEGS
    rows_main = count * MAIN
    rows_all = rows_main + count * EXT
    hid = hidden.shape[1]

    me = lax.axis_index("ctx")
    e_me = me // reps
    r_me = lax.rem(me, reps)
    side = lax.rem(r_me, 2)
    h_me = r_me // 2

    def device(e, h, s):
        return e * reps + h * 2 + s

    def place(e, h, s):
        return (s * halves + h) * experts + e

    def e_fwd(i):
        return lax.rem(e_me + i, experts)

    def e_back(i):
        return lax.rem(e_me + experts - i, experts)

    def h_fwd(j):
        return lax.rem(h_me + j, halves)

    def h_back(j):
        return lax.rem(h_me + halves - j, halves)

    def target(e, h, s):
        return (lax.axis_index("groups"), device(e, h, s))

    weight_copies = [
        pltpu.make_async_copy(src.at[0], dst, weight_sem.at[n])
        for n, (src, dst) in enumerate(((w_gate, gate_w), (w_up, up_w), (w_down, down_w)))
    ]

    barrier = pltpu.get_barrier_semaphore()
    partners = [target(e_fwd(i), h_me, side) for i in range(1, experts)]
    partners += [target(e_me, h_fwd(j), side) for j in range(1, halves)]
    partners += [target(e_me, h_me, 1 - side)]
    for partner in partners:
        pl.semaphore_signal(barrier, inc=1, device_id=partner, device_id_type=MESH)

    mine = place(e_me, h_me, side)
    own_rows = pl.ds(pl.multiple_of(mine * tokens, tokens), tokens)
    kv[own_rows, :kv_width] = keys[...]
    kv[own_rows, kv_width:] = values[...]
    pl.semaphore_wait(barrier, len(partners))

    def remote(src, dst, sems, at, to):
        return pltpu.make_async_remote_copy(
            src_ref=src,
            dst_ref=dst,
            send_sem=sems.at[(0,) + at],
            recv_sem=sems.at[(1,) + at],
            device_id=to,
            device_id_type=MESH,
        )

    def first(use, block, source, i):
        return remote(source(e_fwd(i)), block(mine), group_sem, (use, 0, i), target(e_fwd(i), h_me, side))

    def first_in(use, block, i):
        ref = block(place(e_back(i), h_me, side))
        return remote(ref, ref, group_sem, (use, 0, i), target(e_back(i), h_me, side))

    def second(use, block, j, i):
        ref = block(place(e_back(i), h_me, side))
        return remote(ref, ref, group_sem, (use, j, i), target(e_me, h_fwd(j), side))

    def second_in(use, block, j, i):
        ref = block(place(e_back(i), h_back(j), side))
        return remote(ref, ref, group_sem, (use, j, i), target(e_me, h_back(j), side))

    def third(use, block, j, i):
        ref = block(place(e_back(i), h_back(j), side))
        return remote(ref, ref, pair_sem, (use, j, i), target(e_me, h_me, 1 - side))

    def third_in(use, block, j, i):
        ref = block(place(e_back(i), h_back(j), 1 - side))
        return remote(ref, ref, pair_sem, (use, j, i), target(e_me, h_me, 1 - side))

    def start_first(use, block, source):
        for i in range(1, experts):
            first(use, block, source, i).start()
        pass_on(use, block, 0)

    def pass_on(use, block, i):
        for j in range(1, halves):
            second(use, block, j, i).start()
        third(use, block, 0, i).start()

    def forward_first(use, block, i):
        first_in(use, block, i).wait_recv()
        pass_on(use, block, i)

    def forward_second(use, block, i):
        for j in range(1, halves):
            second_in(use, block, j, i).wait_recv()
            third(use, block, j, i).start()

    def arrive(use, block):
        for i in range(experts):
            for j in range(halves):
                third_in(use, block, j, i).wait_recv()

    def sent(use, block, source):
        for i in range(1, experts):
            first(use, block, source, i).wait_send()
        for i in range(experts):
            for j in range(1, halves):
                second(use, block, j, i).wait_send()
            for j in range(halves):
                third(use, block, j, i).wait_send()

    def kv_block(p):
        return kv.at[pl.ds(pl.multiple_of(p * tokens, tokens), tokens)]

    def kv_source(e):
        return kv_block(mine)

    start_first(0, kv_block, kv_source)
    for copy in weight_copies:
        copy.start()

    key_count = count * tokens
    column = iota((1, key_count), 1)
    key_pos = lax.rem(column, half_rows)
    key_half = column // half_rows
    for s in range(2):
        for h in range(halves):
            for e in range(experts):
                for b in range(2):
                    start = order[2 * (e * reps + h * 2 + s) + b] * half_rows
                    at = 2 * ((s * halves + h) * experts + e) + b
                    key_pos = key_pos + jnp.where(key_half == at, start, 0)
    together = math.gcd(group, max(1, group * 1024 // key_count))
    row = lax.rem(iota((together * tokens, 1), 0), tokens)
    query_pos = lax.rem(row, half_rows) + half_rows * jnp.where(
        row < half_rows, order[2 * me], order[2 * me + 1]
    )

    for i in range(1, experts):
        forward_first(0, kv_block, i)
        forward_second(0, kv_block, i - 1)
    forward_second(0, kv_block, experts - 1)
    arrive(0, kv_block)

    scale = 1.0 / math.sqrt(HEAD_DIM)

    @pl.loop(0, kv_heads * (group // together))
    def _(step):
        k = step // (group // together)
        lanes = together * HEAD_DIM
        q_lanes = pl.ds(pl.multiple_of(step * lanes, lanes), lanes)
        q = fold(queries[:, q_lanes], together)
        key = kv[:, pl.ds(pl.multiple_of(k * HEAD_DIM, HEAD_DIM), HEAD_DIM)]
        value = kv[:, pl.ds(pl.multiple_of(kv_width + k * HEAD_DIM, HEAD_DIM), HEAD_DIM)]
        scores = jnp.where(query_pos >= key_pos, dot_lanes(q, key) * scale, F32(-1e30))
        weights = jnp.exp(scores - jnp.max(scores, axis=1, keepdims=True))
        total_weight = jnp.sum(weights, axis=1, keepdims=True)
        out = dot(weights.astype(BF), value) / total_weight
        attended[:, q_lanes] = unfold(out, together).astype(BF)

    stream = residual[...].astype(F32) + attended[...].astype(F32)
    normed = (
        stream * lax.rsqrt(jnp.mean(stream * stream, axis=1, keepdims=True) + 1e-05)
    ).astype(BF)
    expert_of = ids[...]
    hits = expert_of == iota((tokens, experts), 1)
    before = (iota((tokens, tokens), 0) > iota((tokens, tokens), 1)).astype(F32).astype(BF)
    earlier = dot(before, hits.astype(F32).astype(BF))
    rank = jnp.sum(jnp.where(hits, earlier, 0.0), axis=1, keepdims=True).astype(jnp.int32)
    slot_rows = experts * MAIN
    slot = iota((tokens, slot_rows), 1)
    put_main = (
        ((slot // MAIN == expert_of) & (lax.rem(slot, MAIN) == rank)).astype(F32).astype(BF)
    )
    tall_slot = iota((SEGS * tokens, slot_rows), 1)
    tall_piece = iota((SEGS * tokens, slot_rows), 0) // tokens
    tall_expert = jnp.concatenate([expert_of] * SEGS, axis=0)
    tall_rank = jnp.concatenate([rank] * SEGS, axis=0)
    put_ext = (
        (
            (tall_slot // MAIN == tall_expert)
            & (lax.rem(tall_slot, MAIN) // SEGS + MAIN == tall_rank)
            & (lax.rem(tall_slot, SEGS) == tall_piece)
        )
        .astype(F32)
        .astype(BF)
    )

    def list_block(c):
        return lambda p: lists.at[c, pl.ds(pl.multiple_of(p * MAIN, MAIN), MAIN)]

    def list_source(c):
        return lambda e: outbox.at[c, pl.ds(pl.multiple_of(e * MAIN, MAIN), MAIN)]

    for c in range(CHUNKS):
        piece = normed[:, c * chunk : (c + 1) * chunk]
        outbox[c, :, :chunk] = dot_rows(put_main, piece).astype(BF)
        outbox[c, :, chunk:] = dot_rows(put_ext, fold(piece, SEGS)).astype(BF)
        lists[c, pl.ds(pl.multiple_of(mine * MAIN, MAIN), MAIN)] = outbox[
            c, pl.ds(pl.multiple_of(e_me * MAIN, MAIN), MAIN)
        ]
        start_first(1 + c, list_block(c), list_source(c))

    logits = dot_lanes(normed, router_t[...])
    chosen = jnp.sum(jnp.where(hits, logits, F32(0.0)), axis=1, keepdims=True)
    gates = 1.0 / jnp.sum(jnp.exp(logits - chosen), axis=1, keepdims=True)

    ext_rows = count * EXT
    ext_row = lax.rem(iota((SEGS * ext_rows, rows_main), 0), ext_rows)
    ext_piece = iota((SEGS * ext_rows, rows_main), 0) // ext_rows
    ext_from = (ext_row // EXT) * MAIN + lax.rem(ext_row, EXT) * SEGS + ext_piece
    pick_ext = (iota((SEGS * ext_rows, rows_main), 1) == ext_from).astype(F32).astype(BF)

    tile = min(256, hid)

    def forward_lists(c):
        for i in range(1, experts):
            forward_first(1 + c, list_block(c), i)

    def forward_lists_on(c):
        for i in range(experts):
            forward_second(1 + c, list_block(c), i)

    def multiply(c):
        arrive(1 + c, list_block(c))
        tail = dot(pick_ext, lists[c, :rows_main, chunk:]).astype(BF)
        lists[c, rows_main:, :chunk] = unfold(tail, SEGS)
        depth = pl.ds(c * chunk, chunk)

        @pl.loop(0, hid // tile)
        def _(t):
            cols = pl.ds(pl.multiple_of(t * tile, tile), tile)
            x = lists[c, :, :chunk]
            g = dot(x, gate_w[depth, cols])
            u = dot(x, up_w[depth, cols])
            if c > 0:
                g = g + gated[:, cols]
                u = u + upper[:, cols]
            if c < CHUNKS - 1:
                gated[:, cols] = g
                upper[:, cols] = u
            else:
                hidden[:, cols] = (g / (1.0 + jnp.exp(-g)) * u).astype(BF)

    forward_lists(0)
    forward_lists_on(0)
    forward_lists(1)
    weight_copies[0].wait()
    weight_copies[1].wait()
    multiply(0)
    forward_lists_on(1)
    forward_lists(2)
    multiply(1)
    forward_lists_on(2)
    multiply(2)
    weight_copies[2].wait()

    half_main = rows_main // 2
    group_rows = experts * MAIN
    other_rows = pl.ds(pl.multiple_of((1 - side) * half_main, half_main), half_main)

    def back_pair(c):
        return remote(
            part.at[c, other_rows],
            from_pair.at[c],
            back_pair_sem,
            (c,),
            target(e_me, h_me, 1 - side),
        )

    def back_group(c, j):
        return remote(
            to_group.at[c, j - 1],
            from_group.at[c, j - 1],
            back_group_sem,
            (c, j),
            target(e_me, h_fwd(j), side),
        )

    def back(c, i):
        return remote(
            total.at[c, pl.ds(pl.multiple_of(e_fwd(i) * MAIN, MAIN), MAIN)],
            final.at[c, pl.ds(pl.multiple_of(e_me * MAIN, MAIN), MAIN)],
            back_sem,
            (c, i),
            target(e_fwd(i), h_me, side),
        )

    def produce(c):
        y = dot(hidden[...], down_w[:, c * chunk : (c + 1) * chunk]).astype(BF)
        part[c, :, :chunk] = y[:rows_main]
        part[c, :, chunk:] = dot_rows(pick_ext, fold(y[rows_main:], SEGS)).astype(BF)
        back_pair(c).start()

    def own_sum(c, h):
        rows_here = pl.ds(
            pl.multiple_of(side * half_main + h * group_rows, group_rows), group_rows
        )
        rows_there = pl.ds(pl.multiple_of(h * group_rows, group_rows), group_rows)
        return part[c, rows_here].astype(F32) + from_pair[c, rows_there].astype(F32)

    def reduce_pair(c):
        back_pair(c).wait_recv()
        for j in range(1, halves):
            to_group[c, j - 1] = own_sum(c, h_fwd(j)).astype(BF)
            back_group(c, j).start()

    def reduce_group(c):
        acc = own_sum(c, h_me)
        for j in range(1, halves):
            back_group(c, j).wait_recv()
            acc = acc + from_group[c, j - 1].astype(F32)
        total[c] = acc.astype(BF)
        for i in range(1, experts):
            back(c, i).start()
        mine_rows = pl.ds(pl.multiple_of(e_me * MAIN, MAIN), MAIN)
        final[c, mine_rows] = total[c, mine_rows]

    def finish(c):
        for i in range(1, experts):
            back(c, i).wait_recv()
        main = dot(put_main, final[c, :, :chunk])
        tail = unfold(dot(put_ext, final[c, :, chunk:]), SEGS)
        mixed[:, c * chunk : (c + 1) * chunk] = (gates * (main + tail)).astype(BF)

    produce(0)
    produce(1)
    reduce_pair(0)
    produce(2)
    reduce_pair(1)
    reduce_group(0)
    reduce_pair(2)
    reduce_group(1)
    reduce_group(2)
    for c in range(CHUNKS):
        finish(c)

    sent(0, kv_block, kv_source)
    for c in range(CHUNKS):
        sent(1 + c, list_block(c), list_source(c))
        back_pair(c).wait_send()
        for j in range(1, halves):
            back_group(c, j).wait_send()
        for i in range(1, experts):
            back(c, i).wait_send()


def per_device(
    residual, queries, keys, values, block_order, expert_ids, router, w_gate, w_up, w_down
):
    count = lax.axis_size("ctx")
    experts = router.shape[1]
    reps = count // experts
    halves = reps // 2
    tokens, width = queries.shape
    kv_width = keys.shape[1]
    hid = w_gate.shape[2]
    chunk = width // CHUNKS
    packed = chunk + chunk // SEGS
    rows_main = count * MAIN
    rows_all = rows_main + count * EXT
    group_rows = experts * MAIN
    vmem = pl.BlockSpec(memory_space=pltpu.VMEM)
    smem = pl.BlockSpec(memory_space=pltpu.SMEM)
    hbm = pl.BlockSpec(memory_space=pl.ANY)
    dma = pltpu.SemaphoreType.DMA
    out = jax.ShapeDtypeStruct((tokens, width), BF)
    return pl.pallas_call(
        functools.partial(kernel, count, experts),
        out_shape=(out, out),
        in_specs=[vmem, vmem, vmem, vmem, smem, vmem, vmem, hbm, hbm, hbm],
        out_specs=(vmem, vmem),
        scratch_shapes=[
            pltpu.VMEM((width, hid), BF),
            pltpu.VMEM((width, hid), BF),
            pltpu.VMEM((hid, width), BF),
            pltpu.VMEM((count * tokens, 2 * kv_width), BF),
            pltpu.VMEM((CHUNKS, group_rows, packed), BF),
            pltpu.VMEM((CHUNKS, rows_all, packed), BF),
            pltpu.VMEM((rows_all, hid), F32),
            pltpu.VMEM((rows_all, hid), F32),
            pltpu.VMEM((rows_all, hid), BF),
            pltpu.VMEM((CHUNKS, rows_main, packed), BF),
            pltpu.VMEM((CHUNKS, rows_main // 2, packed), BF),
            pltpu.VMEM((CHUNKS, halves - 1, group_rows, packed), BF),
            pltpu.VMEM((CHUNKS, halves - 1, group_rows, packed), BF),
            pltpu.VMEM((CHUNKS, group_rows, packed), BF),
            pltpu.VMEM((CHUNKS, group_rows, packed), BF),
            dma((3,)),
            dma((2, 1 + CHUNKS, halves, experts)),
            dma((2, 1 + CHUNKS, halves, experts)),
            dma((2, CHUNKS)),
            dma((2, CHUNKS, halves)),
            dma((2, CHUNKS, experts)),
        ],
        compiler_params=pltpu.CompilerParams(
            collective_id=0, has_side_effects=True, vmem_limit_bytes=62 * 1024 * 1024
        ),
        cost_estimate=pl.CostEstimate(
            flops=6 * rows_all * width * hid,
            bytes_accessed=6 * width * hid,
            transcendentals=tokens * width * count,
        ),
    )(
        residual,
        queries,
        keys,
        values,
        block_order,
        expert_ids,
        router.T,
        w_gate,
        w_up,
        w_down,
    )


def solution(mesh):
    return jax.shard_map(
        per_device,
        mesh=mesh,
        in_specs=(
            P(("groups", "ctx"), None),
            P(("groups", "ctx"), None),
            P(("groups", "ctx"), None),
            P(("groups", "ctx"), None),
            P("groups"),
            P(("groups", "ctx"), None),
            P(),
            P("ctx", None, None),
            P("ctx", None, None),
            P("ctx", None, None),
        ),
        out_specs=(P(("groups", "ctx"), None), P(("groups", "ctx"), None)),
        check_vma=False,
    )
```

```python
import functools
import math

import jax
import jax.numpy as jnp
from jax import lax
from jax.experimental import pallas as pl
from jax.experimental.pallas import tpu as pltpu
from jax.sharding import PartitionSpec as P

HEAD_DIM = 128
MOST = 18
MAIN = 16
EXT = MOST - MAIN
SEGS = MAIN // EXT
CHUNKS = 3
MESH = pl.DeviceIdType.MESH
BF = jnp.bfloat16
F32 = jnp.float32


def dot(a, b):
    return jnp.dot(a, b, preferred_element_type=F32)


def dot_rows(a, b):
    return lax.dot_general(a, b, (((0,), (0,)), ((), ())), preferred_element_type=F32)


def dot_lanes(a, b):
    return lax.dot_general(a, b, (((1,), (1,)), ((), ())), preferred_element_type=F32)


def iota(shape, axis):
    return lax.broadcasted_iota(jnp.int32, shape, axis)


def fold(wide, pieces):
    width = wide.shape[1] // pieces
    return jnp.concatenate([wide[:, j * width : (j + 1) * width] for j in range(pieces)], axis=0)


def unfold(tall, pieces):
    rows = tall.shape[0] // pieces
    return jnp.concatenate([tall[j * rows : (j + 1) * rows] for j in range(pieces)], axis=1)


def kernel(
    count,
    experts,
    residual,
    queries,
    keys,
    values,
    order,
    ids,
    router_t,
    w_gate,
    w_up,
    w_down,
    attended,
    mixed,
    gate_w,
    up_w,
    down_w,
    kv,
    key_pos,
    stats,
    summed,
    outbox,
    lists,
    gated,
    upper,
    hidden,
    part,
    from_pair,
    to_group,
    from_group,
    total,
    final,
    weight_sem,
    group_sem,
    pair_sem,
    back_pair_sem,
    back_group_sem,
    back_sem,
):
    tokens, width = queries.shape
    kv_width = keys.shape[1]
    kv_heads = kv_width // HEAD_DIM
    group = width // kv_width
    half_rows = tokens // 2
    reps = count // experts
    halves = reps // 2
    chunk = width // CHUNKS
    seg = chunk // SEGS
    rows_main = count * MAIN
    rows_all = rows_main + count * EXT
    hid = hidden.shape[1]

    me = lax.axis_index("ctx")
    e_me = me // reps
    r_me = lax.rem(me, reps)
    side = lax.rem(r_me, 2)
    h_me = r_me // 2

    def device(e, h, s):
        return e * reps + h * 2 + s

    def place(e, h, s):
        return (s * halves + h) * experts + e

    paired = experts & (experts - 1) == 0

    def e_paired(i):
        out = e_me
        for b in range(i.bit_length()):
            if (i >> b) & 1:
                out = out + (1 << b) * (1 - 2 * lax.rem(e_me // (1 << b), 2))
        return out

    def e_fwd(i):
        return e_paired(i) if paired else lax.rem(e_me + i, experts)

    def e_back(i):
        return e_paired(i) if paired else lax.rem(e_me + experts - i, experts)

    def h_fwd(j):
        return lax.rem(h_me + j, halves)

    def h_back(j):
        return lax.rem(h_me + halves - j, halves)

    def target(e, h, s):
        return (lax.axis_index("groups"), device(e, h, s))

    weight_copies = [
        pltpu.make_async_copy(src.at[0], dst, weight_sem.at[n])
        for n, (src, dst) in enumerate(((w_gate, gate_w), (w_up, up_w), (w_down, down_w)))
    ]

    barrier = pltpu.get_barrier_semaphore()
    partners = [target(e_fwd(i), h_me, side) for i in range(1, experts)]
    partners += [target(e_me, h_fwd(j), side) for j in range(1, halves)]
    partners += [target(e_me, h_me, 1 - side)]
    for partner in partners:
        pl.semaphore_signal(barrier, inc=1, device_id=partner, device_id_type=MESH)

    own_rows = pl.ds(pl.multiple_of(me * tokens, tokens), tokens)
    kv[own_rows, :kv_width] = keys[...]
    kv[own_rows, kv_width:] = values[...]
    pl.semaphore_wait(barrier, len(partners))

    def remote(src, dst, sems, at, to):
        return pltpu.make_async_remote_copy(
            src_ref=src,
            dst_ref=dst,
            send_sem=sems.at[(0,) + at],
            recv_sem=sems.at[(1,) + at],
            device_id=to,
            device_id_type=MESH,
        )

    def first(use, block, source, i):
        return remote(source(e_fwd(i)), block(e_me, h_me, side), group_sem, (use, 0, i), target(e_fwd(i), h_me, side))

    def first_in(use, block, i):
        ref = block(e_back(i), h_me, side)
        return remote(ref, ref, group_sem, (use, 0, i), target(e_back(i), h_me, side))

    def second(use, block, j, i):
        ref = block(e_back(i), h_me, side)
        return remote(ref, ref, group_sem, (use, j, i), target(e_me, h_fwd(j), side))

    def second_in(use, block, j, i):
        ref = block(e_back(i), h_back(j), side)
        return remote(ref, ref, group_sem, (use, j, i), target(e_me, h_back(j), side))

    def third(use, block, j, i):
        ref = block(e_back(i), h_back(j), side)
        return remote(ref, ref, pair_sem, (use, j, i), target(e_me, h_me, 1 - side))

    def third_in(use, block, j, i):
        ref = block(e_back(i), h_back(j), 1 - side)
        return remote(ref, ref, pair_sem, (use, j, i), target(e_me, h_me, 1 - side))

    def start_first(use, block, source):
        for i in range(1, experts):
            first(use, block, source, i).start()
        pass_on(use, block, 0)

    def pass_on(use, block, i):
        for j in range(1, halves):
            second(use, block, j, i).start()
        third(use, block, 0, i).start()

    def forward_first(use, block, i):
        first_in(use, block, i).wait_recv()
        pass_on(use, block, i)

    def forward_second(use, block, i):
        for j in range(1, halves):
            second_in(use, block, j, i).wait_recv()
            third(use, block, j, i).start()

    def arrive(use, block, i):
        for j in range(halves):
            third_in(use, block, j, i).wait_recv()

    def sent(use, block, source):
        for i in range(1, experts):
            first(use, block, source, i).wait_send()
        for i in range(experts):
            for j in range(1, halves):
                second(use, block, j, i).wait_send()
            for j in range(halves):
                third(use, block, j, i).wait_send()

    def kv_block(e, h, s):
        return kv.at[pl.ds(pl.multiple_of(device(e, h, s) * tokens, tokens), tokens)]

    def kv_source(e):
        return kv_block(e_me, h_me, side)

    start_first(0, kv_block, kv_source)
    for copy in weight_copies:
        copy.start()

    plane = reps * tokens
    lane = iota((experts, plane), 1)
    key_half = iota((experts, plane), 0) * (2 * reps) + lane // half_rows
    positions = lax.rem(lane, half_rows)
    for at in range(2 * count):
        positions = positions + jnp.where(key_half == at, order[at] * half_rows, 0)
    key_pos[...] = positions
    row = lax.rem(iota((group * tokens, 1), 0), tokens)
    query_pos = lax.rem(row, half_rows) + half_rows * jnp.where(
        row < half_rows, order[2 * me], order[2 * me + 1]
    )
    scale = 1.0 / math.sqrt(HEAD_DIM)

    def attend(i):
        e = e_back(i)
        rows = pl.ds(pl.multiple_of(e * plane, plane), plane)
        keep = query_pos >= key_pos[pl.ds(e, 1), :]

        @pl.loop(0, kv_heads)
        def _(step):
            lanes = group * HEAD_DIM
            q_lanes = pl.ds(pl.multiple_of(step * lanes, lanes), lanes)
            q = fold(queries[:, q_lanes], group)
            key = kv[rows, pl.ds(pl.multiple_of(step * HEAD_DIM, HEAD_DIM), HEAD_DIM)]
            value = kv[rows, pl.ds(pl.multiple_of(kv_width + step * HEAD_DIM, HEAD_DIM), HEAD_DIM)]
            scores = jnp.where(keep, dot_lanes(q, key) * scale, F32(-1e30))
            top = jnp.max(scores, axis=1, keepdims=True)
            if i > 0:
                top = jnp.maximum(top, stats[step, :, :1])
            weights = jnp.exp(scores - top)
            weight_sum = jnp.sum(weights, axis=1, keepdims=True)
            out = dot(weights.astype(BF), value)
            if i > 0:
                shrink = jnp.exp(stats[step, :, :1] - top)
                weight_sum = weight_sum + shrink * stats[step, :, 1:]
                out = out + shrink * summed[step]
            if i < experts - 1:
                stats[step, :, :1] = top
                stats[step, :, 1:] = weight_sum
                summed[step] = out
            else:
                attended[:, q_lanes] = unfold(out / weight_sum, group).astype(BF).astype(F32)

    for i in range(experts):
        if i + 1 < experts:
            forward_first(0, kv_block, i + 1)
        forward_second(0, kv_block, i)
        if i > 0:
            arrive(0, kv_block, i - 1)
            attend(i - 1)
    arrive(0, kv_block, experts - 1)
    attend(experts - 1)

    stream = residual[...].astype(F32) + attended[...]
    normed = (
        stream * lax.rsqrt(jnp.mean(stream * stream, axis=1, keepdims=True) + 1e-05)
    ).astype(BF)
    ids_here = iota((tokens, tokens), 0) == iota((tokens, tokens), 1)
    expert_of = jnp.sum(jnp.where(ids_here, ids[...], 0).astype(F32), axis=1, keepdims=True)
    expert_of = expert_of.astype(jnp.int32)
    hits = expert_of == iota((tokens, experts), 1)
    before = (iota((tokens, tokens), 0) > iota((tokens, tokens), 1)).astype(F32).astype(BF)
    earlier = dot(before, hits.astype(F32).astype(BF))
    rank = jnp.sum(jnp.where(hits, earlier, 0.0), axis=1, keepdims=True).astype(jnp.int32)
    slot_rows = experts * MAIN
    slot = iota((tokens, slot_rows), 1)
    put_main = (
        ((slot // MAIN == expert_of) & (lax.rem(slot, MAIN) == rank)).astype(F32).astype(BF)
    )
    tall_slot = iota((SEGS * tokens, slot_rows), 1)
    tall_piece = iota((SEGS * tokens, slot_rows), 0) // tokens
    tall_expert = jnp.concatenate([expert_of] * SEGS, axis=0)
    tall_rank = jnp.concatenate([rank] * SEGS, axis=0)
    put_ext = (
        (
            (tall_slot // MAIN == tall_expert)
            & (lax.rem(tall_slot, MAIN) // SEGS + MAIN == tall_rank)
            & (lax.rem(tall_slot, SEGS) == tall_piece)
        )
        .astype(F32)
        .astype(BF)
    )

    def list_block(c):
        return lambda e, h, s: lists.at[
            c, pl.ds(pl.multiple_of(place(e, h, s) * MAIN, MAIN), MAIN)
        ]

    def list_source(c):
        return lambda e: outbox.at[c, pl.ds(pl.multiple_of(e * MAIN, MAIN), MAIN)]

    for c in range(CHUNKS):
        piece = normed[:, c * chunk : (c + 1) * chunk]
        outbox[c, :, :chunk] = dot_rows(put_main, piece).astype(BF)
        outbox[c, :, chunk:] = dot_rows(put_ext, fold(piece, SEGS)).astype(BF)
        lists[c, pl.ds(pl.multiple_of(place(e_me, h_me, side) * MAIN, MAIN), MAIN)] = outbox[
            c, pl.ds(pl.multiple_of(e_me * MAIN, MAIN), MAIN)
        ]
        start_first(1 + c, list_block(c), list_source(c))

    logits = dot_lanes(normed, router_t[...])
    chosen = jnp.sum(jnp.where(hits, logits, F32(0.0)), axis=1, keepdims=True)
    gates = 1.0 / jnp.sum(jnp.exp(logits - chosen), axis=1, keepdims=True)

    ext_rows = count * EXT
    ext_row = lax.rem(iota((SEGS * ext_rows, rows_main), 0), ext_rows)
    ext_piece = iota((SEGS * ext_rows, rows_main), 0) // ext_rows
    ext_from = (ext_row // EXT) * MAIN + lax.rem(ext_row, EXT) * SEGS + ext_piece
    pick_ext = (iota((SEGS * ext_rows, rows_main), 1) == ext_from).astype(F32).astype(BF)

    tile = min(256, hid)

    def forward_lists(c):
        for i in range(1, experts):
            forward_first(1 + c, list_block(c), i)

    def forward_lists_on(c):
        for i in range(experts):
            forward_second(1 + c, list_block(c), i)

    def multiply(c):
        for i in range(experts):
            arrive(1 + c, list_block(c), i)
        tail = dot(pick_ext, lists[c, :rows_main, chunk:]).astype(BF)
        lists[c, rows_main:, :chunk] = unfold(tail, SEGS)
        depth = pl.ds(c * chunk, chunk)

        @pl.loop(0, hid // tile)
        def _(t):
            cols = pl.ds(pl.multiple_of(t * tile, tile), tile)
            x = lists[c, :, :chunk]
            g = dot(x, gate_w[depth, cols])
            u = dot(x, up_w[depth, cols])
            if c > 0:
                g = g + gated[:, cols]
                u = u + upper[:, cols]
            if c < CHUNKS - 1:
                gated[:, cols] = g
                upper[:, cols] = u
            else:
                hidden[:, cols] = (g / (1.0 + jnp.exp(-g)) * u).astype(BF)

    forward_lists(0)
    forward_lists(1)
    forward_lists_on(0)
    forward_lists(2)
    weight_copies[0].wait()
    weight_copies[1].wait()
    multiply(0)
    forward_lists_on(1)
    multiply(1)
    forward_lists_on(2)
    multiply(2)
    weight_copies[2].wait()

    half_main = rows_main // 2
    group_rows = experts * MAIN
    other_rows = pl.ds(pl.multiple_of((1 - side) * half_main, half_main), half_main)

    def back_pair(c):
        return remote(
            part.at[c, other_rows],
            from_pair.at[c],
            back_pair_sem,
            (c,),
            target(e_me, h_me, 1 - side),
        )

    def block_rows(start, e):
        return pl.ds(pl.multiple_of(start + e * MAIN, MAIN), MAIN)

    def back_group(c, j, i):
        rows = block_rows(0, e_fwd(i))
        return remote(
            to_group.at[c, j - 1, rows],
            from_group.at[c, j - 1, rows],
            back_group_sem,
            (c, j, i),
            target(e_me, h_fwd(j), side),
        )

    def back_group_in(c, j, i):
        ref = from_group.at[c, j - 1, block_rows(0, e_fwd(i))]
        return remote(ref, ref, back_group_sem, (c, j, i), target(e_me, h_back(j), side))

    def back(c, i):
        return remote(
            total.at[c, pl.ds(pl.multiple_of(e_fwd(i) * MAIN, MAIN), MAIN)],
            final.at[c, pl.ds(pl.multiple_of(e_me * MAIN, MAIN), MAIN)],
            back_sem,
            (c, i),
            target(e_fwd(i), h_me, side),
        )

    def produce(c):
        y = dot(hidden[...], down_w[:, c * chunk : (c + 1) * chunk]).astype(BF)
        part[c, :, :chunk] = y[:rows_main]
        part[c, :, chunk:] = dot_rows(pick_ext, fold(y[rows_main:], SEGS)).astype(BF)
        back_pair(c).start()

    turns = list(range(1, experts)) + [0]

    def own_sum(c, h, e):
        here = part[c, block_rows(side * half_main + h * group_rows, e)]
        return here.astype(F32) + from_pair[c, block_rows(h * group_rows, e)].astype(F32)

    def reduce_pair(c):
        back_pair(c).wait_recv()
        for i in turns:
            for j in range(1, halves):
                e = e_fwd(i)
                to_group[c, j - 1, block_rows(0, e)] = own_sum(c, h_fwd(j), e).astype(BF)
                back_group(c, j, i).start()

    def reduce_group(c):
        for i in turns:
            e = e_fwd(i)
            acc = own_sum(c, h_me, e)
            for j in range(1, halves):
                back_group_in(c, j, i).wait_recv()
                acc = acc + from_group[c, j - 1, block_rows(0, e)].astype(F32)
            if i > 0:
                total[c, block_rows(0, e)] = acc.astype(BF)
                back(c, i).start()
            else:
                final[c, block_rows(0, e)] = acc.astype(BF)

    def finish(c):
        for i in range(1, experts):
            back(c, i).wait_recv()
        main = dot(put_main, final[c, :, :chunk])
        tail = unfold(dot(put_ext, final[c, :, chunk:]), SEGS)
        mixed[:, c * chunk : (c + 1) * chunk] = gates * (main + tail)

    produce(0)
    produce(1)
    reduce_pair(0)
    produce(2)
    reduce_pair(1)
    reduce_group(0)
    reduce_pair(2)
    reduce_group(1)
    reduce_group(2)
    for c in range(CHUNKS):
        finish(c)

    sent(0, kv_block, kv_source)
    for c in range(CHUNKS):
        sent(1 + c, list_block(c), list_source(c))
        back_pair(c).wait_send()
        for j in range(1, halves):
            for i in range(experts):
                back_group(c, j, i).wait_send()
        for i in range(1, experts):
            back(c, i).wait_send()


def per_device(
    residual, queries, keys, values, block_order, expert_ids, router, w_gate, w_up, w_down
):
    count = lax.axis_size("ctx")
    experts = router.shape[1]
    reps = count // experts
    halves = reps // 2
    tokens, width = queries.shape
    kv_width = keys.shape[1]
    hid = w_gate.shape[2]
    group = width // kv_width
    chunk = width // CHUNKS
    packed = chunk + chunk // SEGS
    rows_main = count * MAIN
    rows_all = rows_main + count * EXT
    group_rows = experts * MAIN
    vmem = pl.BlockSpec(memory_space=pltpu.VMEM)
    smem = pl.BlockSpec(memory_space=pltpu.SMEM)
    hbm = pl.BlockSpec(memory_space=pl.ANY)
    dma = pltpu.SemaphoreType.DMA
    out = jax.ShapeDtypeStruct((tokens, width), F32)
    attended, mixed = pl.pallas_call(
        functools.partial(kernel, count, experts),
        out_shape=(out, out),
        in_specs=[vmem, vmem, vmem, vmem, smem, vmem, vmem, hbm, hbm, hbm],
        out_specs=(vmem, vmem),
        scratch_shapes=[
            pltpu.VMEM((width, hid), BF),
            pltpu.VMEM((width, hid), BF),
            pltpu.VMEM((hid, width), BF),
            pltpu.VMEM((count * tokens, 2 * kv_width), BF),
            pltpu.VMEM((experts, reps * tokens), jnp.int32),
            pltpu.VMEM((kv_width // HEAD_DIM, group * tokens, 2), F32),
            pltpu.VMEM((kv_width // HEAD_DIM, group * tokens, HEAD_DIM), F32),
            pltpu.VMEM((CHUNKS, group_rows, packed), BF),
            pltpu.VMEM((CHUNKS, rows_all, packed), BF),
            pltpu.VMEM((rows_all, hid), F32),
            pltpu.VMEM((rows_all, hid), F32),
            pltpu.VMEM((rows_all, hid), BF),
            pltpu.VMEM((CHUNKS, rows_main, packed), BF),
            pltpu.VMEM((CHUNKS, rows_main // 2, packed), BF),
            pltpu.VMEM((CHUNKS, halves - 1, group_rows, packed), BF),
            pltpu.VMEM((CHUNKS, halves - 1, group_rows, packed), BF),
            pltpu.VMEM((CHUNKS, group_rows, packed), BF),
            pltpu.VMEM((CHUNKS, group_rows, packed), BF),
            dma((3,)),
            dma((2, 1 + CHUNKS, halves, experts)),
            dma((2, 1 + CHUNKS, halves, experts)),
            dma((2, CHUNKS)),
            dma((2, CHUNKS, halves, experts)),
            dma((2, CHUNKS, experts)),
        ],
        compiler_params=pltpu.CompilerParams(
            collective_id=0, has_side_effects=True, vmem_limit_bytes=62 * 1024 * 1024
        ),
        cost_estimate=pl.CostEstimate(
            flops=6 * rows_all * width * hid,
            bytes_accessed=6 * width * hid,
            transcendentals=tokens * width * count,
        ),
    )(
        residual,
        queries,
        keys,
        values,
        block_order,
        expert_ids.reshape(1, tokens),
        router.T,
        w_gate,
        w_up,
        w_down,
    )
    return attended.astype(BF), mixed.astype(BF)


def solution(mesh):
    return jax.shard_map(
        per_device,
        mesh=mesh,
        in_specs=(
            P(("groups", "ctx"), None),
            P(("groups", "ctx"), None),
            P(("groups", "ctx"), None),
            P(("groups", "ctx"), None),
            P("groups"),
            P(("groups", "ctx"), None),
            P(),
            P("ctx", None, None),
            P("ctx", None, None),
            P("ctx", None, None),
        ),
        out_specs=(P(("groups", "ctx"), None), P(("groups", "ctx"), None)),
        check_vma=False,
    )
```

```python
import functools
import math

import jax
import jax.numpy as jnp
from jax import lax
from jax.experimental import pallas as pl
from jax.experimental.pallas import tpu as pltpu
from jax.sharding import PartitionSpec as P

HEAD_DIM = 128
MOST = 18
MAIN = 16
EXT = MOST - MAIN
SEGS = MAIN // EXT
CHUNKS = 3
MESH = pl.DeviceIdType.MESH
BF = jnp.bfloat16
F32 = jnp.float32


def dot(a, b):
    return jnp.dot(a, b, preferred_element_type=F32)


def dot_rows(a, b):
    return lax.dot_general(a, b, (((0,), (0,)), ((), ())), preferred_element_type=F32)


def dot_lanes(a, b):
    return lax.dot_general(a, b, (((1,), (1,)), ((), ())), preferred_element_type=F32)


def iota(shape, axis):
    return lax.broadcasted_iota(jnp.int32, shape, axis)


def fold(wide, pieces):
    width = wide.shape[1] // pieces
    return jnp.concatenate([wide[:, j * width : (j + 1) * width] for j in range(pieces)], axis=0)


def unfold(tall, pieces):
    rows = tall.shape[0] // pieces
    return jnp.concatenate([tall[j * rows : (j + 1) * rows] for j in range(pieces)], axis=1)


def kernel(
    count,
    experts,
    residual,
    queries,
    keys,
    values,
    order,
    ids,
    router_t,
    w_gate,
    w_up,
    w_down,
    attended,
    mixed,
    gate_w,
    up_w,
    down_w,
    kv,
    outbox,
    lists,
    gated,
    upper,
    hidden,
    part,
    from_pair,
    to_group,
    from_group,
    total,
    final,
    weight_sem,
    group_sem,
    pair_sem,
    back_pair_sem,
    back_group_sem,
    back_sem,
):
    tokens, width = queries.shape
    kv_width = keys.shape[1]
    kv_heads = kv_width // HEAD_DIM
    group = width // kv_width
    half_rows = tokens // 2
    reps = count // experts
    halves = reps // 2
    chunk = width // CHUNKS
    seg = chunk // SEGS
    rows_main = count * MAIN
    rows_all = rows_main + count * EXT
    hid = hidden.shape[1]

    me = lax.axis_index("ctx")
    e_me = me // reps
    r_me = lax.rem(me, reps)
    side = lax.rem(r_me, 2)
    h_me = r_me // 2

    def device(e, h, s):
        return e * reps + h * 2 + s

    def place(e, h, s):
        return (s * halves + h) * experts + e

    def e_fwd(i):
        return lax.rem(e_me + i, experts)

    def e_back(i):
        return lax.rem(e_me + experts - i, experts)

    def h_fwd(j):
        return lax.rem(h_me + j, halves)

    def h_back(j):
        return lax.rem(h_me + halves - j, halves)

    def target(e, h, s):
        return (lax.axis_index("groups"), device(e, h, s))

    weight_copies = [
        pltpu.make_async_copy(src.at[0], dst, weight_sem.at[n])
        for n, (src, dst) in enumerate(((w_gate, gate_w), (w_up, up_w), (w_down, down_w)))
    ]

    barrier = pltpu.get_barrier_semaphore()
    partners = [target(e_fwd(i), h_me, side) for i in range(1, experts)]
    partners += [target(e_me, h_fwd(j), side) for j in range(1, halves)]
    partners += [target(e_me, h_me, 1 - side)]
    for partner in partners:
        pl.semaphore_signal(barrier, inc=1, device_id=partner, device_id_type=MESH)

    mine = place(e_me, h_me, side)
    own_rows = pl.ds(pl.multiple_of(mine * tokens, tokens), tokens)
    kv[own_rows, :kv_width] = keys[...]
    kv[own_rows, kv_width:] = values[...]
    pl.semaphore_wait(barrier, len(partners))

    def remote(src, dst, sems, at, to):
        return pltpu.make_async_remote_copy(
            src_ref=src,
            dst_ref=dst,
            send_sem=sems.at[(0,) + at],
            recv_sem=sems.at[(1,) + at],
            device_id=to,
            device_id_type=MESH,
        )

    def first(use, block, source, i):
        return remote(source(e_fwd(i)), block(mine), group_sem, (use, 0, i), target(e_fwd(i), h_me, side))

    def first_in(use, block, i):
        ref = block(place(e_back(i), h_me, side))
        return remote(ref, ref, group_sem, (use, 0, i), target(e_back(i), h_me, side))

    def second(use, block, j, i):
        ref = block(place(e_back(i), h_me, side))
        return remote(ref, ref, group_sem, (use, j, i), target(e_me, h_fwd(j), side))

    def second_in(use, block, j, i):
        ref = block(place(e_back(i), h_back(j), side))
        return remote(ref, ref, group_sem, (use, j, i), target(e_me, h_back(j), side))

    def third(use, block, j, i):
        ref = block(place(e_back(i), h_back(j), side))
        return remote(ref, ref, pair_sem, (use, j, i), target(e_me, h_me, 1 - side))

    def third_in(use, block, j, i):
        ref = block(place(e_back(i), h_back(j), 1 - side))
        return remote(ref, ref, pair_sem, (use, j, i), target(e_me, h_me, 1 - side))

    def start_first(use, block, source):
        for i in range(1, experts):
            first(use, block, source, i).start()
        pass_on(use, block, 0)

    def pass_on(use, block, i):
        for j in range(1, halves):
            second(use, block, j, i).start()
        third(use, block, 0, i).start()

    def forward_first(use, block, i):
        first_in(use, block, i).wait_recv()
        pass_on(use, block, i)

    def forward_second(use, block, i):
        for j in range(1, halves):
            second_in(use, block, j, i).wait_recv()
            third(use, block, j, i).start()

    def arrive(use, block):
        for i in range(experts):
            for j in range(halves):
                third_in(use, block, j, i).wait_recv()

    def sent(use, block, source):
        for i in range(1, experts):
            first(use, block, source, i).wait_send()
        for i in range(experts):
            for j in range(1, halves):
                second(use, block, j, i).wait_send()
            for j in range(halves):
                third(use, block, j, i).wait_send()

    def kv_block(p):
        return kv.at[pl.ds(pl.multiple_of(p * tokens, tokens), tokens)]

    def kv_source(e):
        return kv_block(mine)

    start_first(0, kv_block, kv_source)
    for copy in weight_copies:
        copy.start()

    key_count = count * tokens
    column = iota((1, key_count), 1)
    key_pos = lax.rem(column, half_rows)
    key_half = column // half_rows
    for s in range(2):
        for h in range(halves):
            for e in range(experts):
                for b in range(2):
                    start = order[2 * (e * reps + h * 2 + s) + b] * half_rows
                    at = 2 * ((s * halves + h) * experts + e) + b
                    key_pos = key_pos + jnp.where(key_half == at, start, 0)
    together = math.gcd(group, max(1, group * 1024 // key_count))
    row = lax.rem(iota((together * tokens, 1), 0), tokens)
    query_pos = lax.rem(row, half_rows) + half_rows * jnp.where(
        row < half_rows, order[2 * me], order[2 * me + 1]
    )

    for i in range(1, experts):
        forward_first(0, kv_block, i)
        forward_second(0, kv_block, i - 1)
    forward_second(0, kv_block, experts - 1)
    arrive(0, kv_block)

    scale = 1.0 / math.sqrt(HEAD_DIM)

    @pl.loop(0, kv_heads * (group // together))
    def _(step):
        k = step // (group // together)
        lanes = together * HEAD_DIM
        q_lanes = pl.ds(pl.multiple_of(step * lanes, lanes), lanes)
        q = fold(queries[:, q_lanes], together)
        key = kv[:, pl.ds(pl.multiple_of(k * HEAD_DIM, HEAD_DIM), HEAD_DIM)]
        value = kv[:, pl.ds(pl.multiple_of(kv_width + k * HEAD_DIM, HEAD_DIM), HEAD_DIM)]
        scores = jnp.where(query_pos >= key_pos, dot_lanes(q, key) * scale, F32(-1e30))
        weights = jnp.exp(scores - jnp.max(scores, axis=1, keepdims=True))
        total_weight = jnp.sum(weights, axis=1, keepdims=True)
        out = dot(weights.astype(BF), value) / total_weight
        attended[:, q_lanes] = unfold(out, together).astype(BF)

    stream = residual[...].astype(F32) + attended[...].astype(F32)
    normed = (
        stream * lax.rsqrt(jnp.mean(stream * stream, axis=1, keepdims=True) + 1e-05)
    ).astype(BF)
    ids_here = iota((tokens, tokens), 0) == iota((tokens, tokens), 1)
    expert_of = jnp.sum(jnp.where(ids_here, ids[...], 0).astype(F32), axis=1, keepdims=True)
    expert_of = expert_of.astype(jnp.int32)
    hits = expert_of == iota((tokens, experts), 1)
    before = (iota((tokens, tokens), 0) > iota((tokens, tokens), 1)).astype(F32).astype(BF)
    earlier = dot(before, hits.astype(F32).astype(BF))
    rank = jnp.sum(jnp.where(hits, earlier, 0.0), axis=1, keepdims=True).astype(jnp.int32)
    slot_rows = experts * MAIN
    slot = iota((tokens, slot_rows), 1)
    put_main = (
        ((slot // MAIN == expert_of) & (lax.rem(slot, MAIN) == rank)).astype(F32).astype(BF)
    )
    tall_slot = iota((SEGS * tokens, slot_rows), 1)
    tall_piece = iota((SEGS * tokens, slot_rows), 0) // tokens
    tall_expert = jnp.concatenate([expert_of] * SEGS, axis=0)
    tall_rank = jnp.concatenate([rank] * SEGS, axis=0)
    put_ext = (
        (
            (tall_slot // MAIN == tall_expert)
            & (lax.rem(tall_slot, MAIN) // SEGS + MAIN == tall_rank)
            & (lax.rem(tall_slot, SEGS) == tall_piece)
        )
        .astype(F32)
        .astype(BF)
    )

    def list_block(c):
        return lambda p: lists.at[c, pl.ds(pl.multiple_of(p * MAIN, MAIN), MAIN)]

    def list_source(c):
        return lambda e: outbox.at[c, pl.ds(pl.multiple_of(e * MAIN, MAIN), MAIN)]

    for c in range(CHUNKS):
        piece = normed[:, c * chunk : (c + 1) * chunk]
        outbox[c, :, :chunk] = dot_rows(put_main, piece).astype(BF)
        outbox[c, :, chunk:] = dot_rows(put_ext, fold(piece, SEGS)).astype(BF)
        lists[c, pl.ds(pl.multiple_of(mine * MAIN, MAIN), MAIN)] = outbox[
            c, pl.ds(pl.multiple_of(e_me * MAIN, MAIN), MAIN)
        ]
        start_first(1 + c, list_block(c), list_source(c))

    logits = dot_lanes(normed, router_t[...])
    chosen = jnp.sum(jnp.where(hits, logits, F32(0.0)), axis=1, keepdims=True)
    gates = 1.0 / jnp.sum(jnp.exp(logits - chosen), axis=1, keepdims=True)

    ext_rows = count * EXT
    ext_row = lax.rem(iota((SEGS * ext_rows, rows_main), 0), ext_rows)
    ext_piece = iota((SEGS * ext_rows, rows_main), 0) // ext_rows
    ext_from = (ext_row // EXT) * MAIN + lax.rem(ext_row, EXT) * SEGS + ext_piece
    pick_ext = (iota((SEGS * ext_rows, rows_main), 1) == ext_from).astype(F32).astype(BF)

    tile = min(256, hid)

    def forward_lists(c):
        for i in range(1, experts):
            forward_first(1 + c, list_block(c), i)

    def forward_lists_on(c):
        for i in range(experts):
            forward_second(1 + c, list_block(c), i)

    def multiply(c):
        arrive(1 + c, list_block(c))
        tail = dot(pick_ext, lists[c, :rows_main, chunk:]).astype(BF)
        lists[c, rows_main:, :chunk] = unfold(tail, SEGS)
        depth = pl.ds(c * chunk, chunk)

        @pl.loop(0, hid // tile)
        def _(t):
            cols = pl.ds(pl.multiple_of(t * tile, tile), tile)
            x = lists[c, :, :chunk]
            g = dot(x, gate_w[depth, cols])
            u = dot(x, up_w[depth, cols])
            if c > 0:
                g = g + gated[:, cols]
                u = u + upper[:, cols]
            if c < CHUNKS - 1:
                gated[:, cols] = g
                upper[:, cols] = u
            else:
                hidden[:, cols] = (g / (1.0 + jnp.exp(-g)) * u).astype(BF)

    forward_lists(0)
    forward_lists(1)
    forward_lists_on(0)
    forward_lists(2)
    weight_copies[0].wait()
    weight_copies[1].wait()
    multiply(0)
    forward_lists_on(1)
    multiply(1)
    forward_lists_on(2)
    multiply(2)
    weight_copies[2].wait()

    half_main = rows_main // 2
    group_rows = experts * MAIN
    other_rows = pl.ds(pl.multiple_of((1 - side) * half_main, half_main), half_main)

    def back_pair(c):
        return remote(
            part.at[c, other_rows],
            from_pair.at[c],
            back_pair_sem,
            (c,),
            target(e_me, h_me, 1 - side),
        )

    def back_group(c, j):
        return remote(
            to_group.at[c, j - 1],
            from_group.at[c, j - 1],
            back_group_sem,
            (c, j),
            target(e_me, h_fwd(j), side),
        )

    def back(c, i):
        return remote(
            total.at[c, pl.ds(pl.multiple_of(e_fwd(i) * MAIN, MAIN), MAIN)],
            final.at[c, pl.ds(pl.multiple_of(e_me * MAIN, MAIN), MAIN)],
            back_sem,
            (c, i),
            target(e_fwd(i), h_me, side),
        )

    def produce(c):
        y = dot(hidden[...], down_w[:, c * chunk : (c + 1) * chunk]).astype(BF)
        part[c, :, :chunk] = y[:rows_main]
        part[c, :, chunk:] = dot_rows(pick_ext, fold(y[rows_main:], SEGS)).astype(BF)
        back_pair(c).start()

    def own_sum(c, h):
        rows_here = pl.ds(
            pl.multiple_of(side * half_main + h * group_rows, group_rows), group_rows
        )
        rows_there = pl.ds(pl.multiple_of(h * group_rows, group_rows), group_rows)
        return part[c, rows_here].astype(F32) + from_pair[c, rows_there].astype(F32)

    def reduce_pair(c):
        back_pair(c).wait_recv()
        for j in range(1, halves):
            to_group[c, j - 1] = own_sum(c, h_fwd(j)).astype(BF)
            back_group(c, j).start()

    def reduce_group(c):
        acc = own_sum(c, h_me)
        for j in range(1, halves):
            back_group(c, j).wait_recv()
            acc = acc + from_group[c, j - 1].astype(F32)
        total[c] = acc.astype(BF)
        for i in range(1, experts):
            back(c, i).start()
        mine_rows = pl.ds(pl.multiple_of(e_me * MAIN, MAIN), MAIN)
        final[c, mine_rows] = total[c, mine_rows]

    def finish(c):
        for i in range(1, experts):
            back(c, i).wait_recv()
        main = dot(put_main, final[c, :, :chunk])
        tail = unfold(dot(put_ext, final[c, :, chunk:]), SEGS)
        mixed[:, c * chunk : (c + 1) * chunk] = (gates * (main + tail)).astype(BF)

    produce(0)
    produce(1)
    reduce_pair(0)
    produce(2)
    reduce_pair(1)
    reduce_group(0)
    reduce_pair(2)
    reduce_group(1)
    reduce_group(2)
    for c in range(CHUNKS):
        finish(c)

    sent(0, kv_block, kv_source)
    for c in range(CHUNKS):
        sent(1 + c, list_block(c), list_source(c))
        back_pair(c).wait_send()
        for j in range(1, halves):
            back_group(c, j).wait_send()
        for i in range(1, experts):
            back(c, i).wait_send()


def per_device(
    residual, queries, keys, values, block_order, expert_ids, router, w_gate, w_up, w_down
):
    count = lax.axis_size("ctx")
    experts = router.shape[1]
    reps = count // experts
    halves = reps // 2
    tokens, width = queries.shape
    kv_width = keys.shape[1]
    hid = w_gate.shape[2]
    chunk = width // CHUNKS
    packed = chunk + chunk // SEGS
    rows_main = count * MAIN
    rows_all = rows_main + count * EXT
    group_rows = experts * MAIN
    vmem = pl.BlockSpec(memory_space=pltpu.VMEM)
    smem = pl.BlockSpec(memory_space=pltpu.SMEM)
    hbm = pl.BlockSpec(memory_space=pl.ANY)
    dma = pltpu.SemaphoreType.DMA
    out = jax.ShapeDtypeStruct((tokens, width), BF)
    return pl.pallas_call(
        functools.partial(kernel, count, experts),
        out_shape=(out, out),
        in_specs=[vmem, vmem, vmem, vmem, smem, vmem, vmem, hbm, hbm, hbm],
        out_specs=(vmem, vmem),
        scratch_shapes=[
            pltpu.VMEM((width, hid), BF),
            pltpu.VMEM((width, hid), BF),
            pltpu.VMEM((hid, width), BF),
            pltpu.VMEM((count * tokens, 2 * kv_width), BF),
            pltpu.VMEM((CHUNKS, group_rows, packed), BF),
            pltpu.VMEM((CHUNKS, rows_all, packed), BF),
            pltpu.VMEM((rows_all, hid), F32),
            pltpu.VMEM((rows_all, hid), F32),
            pltpu.VMEM((rows_all, hid), BF),
            pltpu.VMEM((CHUNKS, rows_main, packed), BF),
            pltpu.VMEM((CHUNKS, rows_main // 2, packed), BF),
            pltpu.VMEM((CHUNKS, halves - 1, group_rows, packed), BF),
            pltpu.VMEM((CHUNKS, halves - 1, group_rows, packed), BF),
            pltpu.VMEM((CHUNKS, group_rows, packed), BF),
            pltpu.VMEM((CHUNKS, group_rows, packed), BF),
            dma((3,)),
            dma((2, 1 + CHUNKS, halves, experts)),
            dma((2, 1 + CHUNKS, halves, experts)),
            dma((2, CHUNKS)),
            dma((2, CHUNKS, halves)),
            dma((2, CHUNKS, experts)),
        ],
        compiler_params=pltpu.CompilerParams(
            collective_id=0, has_side_effects=True, vmem_limit_bytes=62 * 1024 * 1024
        ),
        cost_estimate=pl.CostEstimate(
            flops=6 * rows_all * width * hid,
            bytes_accessed=6 * width * hid,
            transcendentals=tokens * width * count,
        ),
    )(
        residual,
        queries,
        keys,
        values,
        block_order,
        expert_ids.reshape(1, tokens),
        router.T,
        w_gate,
        w_up,
        w_down,
    )


def solution(mesh):
    return jax.shard_map(
        per_device,
        mesh=mesh,
        in_specs=(
            P(("groups", "ctx"), None),
            P(("groups", "ctx"), None),
            P(("groups", "ctx"), None),
            P(("groups", "ctx"), None),
            P("groups"),
            P(("groups", "ctx"), None),
            P(),
            P("ctx", None, None),
            P("ctx", None, None),
            P("ctx", None, None),
        ),
        out_specs=(P(("groups", "ctx"), None), P(("groups", "ctx"), None)),
        check_vma=False,
    )
```
